256 devices in a mesh: ctx: 64 (over x, y, z_hi), head: 4 (over z_lo, core).
Axes of the slice: x: 4, y: 4, z: 8 (z_hi: 4, z_lo: 2; z = z_hi * 2 + z_lo), core: 2. Of those that a mesh axis runs over, the one named last changes fastest.
Arguments:
- mla_query: bfloat16 [8192, 3072], P('ctx', 'head'), may hold values from -8 to 8
- mla_latent: bfloat16 [8192, 576], P(('ctx', 'head')), may hold values from -8 to 8
- kv_gain: float32 [512], replicated, may hold values from 0.1 to 1.9
- w_key_up: bfloat16 [512, 2048], P(None, 'head'), may hold values from -0.25 to 0.25
- w_value_up: bfloat16 [512, 2048], P(None, 'head'), may hold values from -0.25 to 0.25
- w_mla_out: bfloat16 [2048, 2304], P('head'), may hold values from -0.5 to 0.5
- kda_query: bfloat16 [8192, 2048], P('ctx', 'head'), may hold values from -6 to 6
- kda_key: bfloat16 [8192, 2048], P('ctx', 'head'), may hold values from -6 to 6
- kda_value: bfloat16 [8192, 2048], P('ctx', 'head'), may hold values from -6 to 6
- kda_decay: float32 [8192, 2048], P('ctx', 'head'), may hold values from -1 to 0
- kda_beta: float32 [16, 8192], P('head', 'ctx'), may hold values from 0 to 1
- w_kda_out: bfloat16 [2048, 2304], P('head'), may hold values from -0.125 to 0.125
Outputs:
- mla_mixed: bfloat16 [8192, 2304], P('ctx', 'head')
- kda_mixed: bfloat16 [8192, 2304], P('ctx', 'head')
The draws below stay inside these ranges and needn't reach their ends.
All inputs are finite; a program needn't handle non-finite values.
Results may differ from the reference program's by a relative error of at most 0.02.
Values may be sent and summed in bfloat16 or wider, within the bound.
No kernel may reach another device: no remote copies, remote signals or barrier semaphores. Data moves between devices by JAX's collectives and lax.ppermute only.
A program may use at most 128 MiB of HBM per device.

```python
import math
import jax
import jax.numpy as jnp
from jax import lax

D = 2304
HEAD_DIM = 128
KEY_SHARED = 64
RANK = 512
MLA_HEADS = 16
KDA_HEADS = 16
TOK_DEV = 128
PROMPT_SPAN = 8192


def draw_mla_query(key, part):
    key = jax.random.fold_in(key, 5)
    row_width = HEAD_DIM + KEY_SHARED
    array_shape = (PROMPT_SPAN, MLA_HEADS * row_width)
    result = jnp.clip(2.0 * jax.random.normal(key, array_shape, jnp.float32), -8.0, 8.0)
    return result.astype(jnp.bfloat16)


def draw_mla_latent(key, part):
    key = jax.random.fold_in(key, 7)
    array_shape = (PROMPT_SPAN, RANK + KEY_SHARED)
    result = jnp.clip(jax.random.normal(key, array_shape, jnp.float32), -6.0, 6.0)
    return result.astype(jnp.bfloat16)


def draw_kda_decay(key, part):
    key = jax.random.fold_in(key, 11)
    stochastic_seeds = jax.random.split(key, 7)
    feature_slots = KDA_HEADS * HEAD_DIM
    block_count = PROMPT_SPAN // TOK_DEV
    fast_share = 0.5
    forgetful = jax.random.uniform(stochastic_seeds[0], (feature_slots,), jnp.float32) < fast_share
    fast_rate = jnp.exp(jax.random.uniform(stochastic_seeds[1], (feature_slots,), jnp.float32, math.log(1.0 / 50.0), math.log(1.0 / 30.0)))
    slow_rate = jnp.exp(jax.random.uniform(stochastic_seeds[2], (feature_slots,), jnp.float32, math.log(0.05), math.log(0.2))) / PROMPT_SPAN
    base_rate = jnp.where(forgetful, fast_rate, slow_rate)
    device_factor = jnp.exp(jax.random.uniform(stochastic_seeds[3], (block_count, 1, feature_slots), jnp.float32, math.log(0.7), math.log(1.4)))
    roughness = jnp.exp(jax.random.uniform(stochastic_seeds[4], (block_count, TOK_DEV, feature_slots), jnp.float32, math.log(0.5), math.log(1.5)))
    speed_table = (base_rate * device_factor * roughness).reshape(PROMPT_SPAN, feature_slots)
    line_spikes = jax.random.randint(stochastic_seeds[5], (2,), 0, PROMPT_SPAN)
    spike_extent = jnp.log(jax.random.uniform(stochastic_seeds[6], (2, feature_slots), jnp.float32, 0.5, 0.8))
    line_number = jnp.arange(PROMPT_SPAN, dtype=jnp.int32)[:, None]
    spike_clusters = jnp.where(line_number == line_spikes[0], spike_extent[0][None, :], 0.0)
    spike_clusters = spike_clusters + jnp.where(line_number == line_spikes[1], spike_extent[1][None, :], 0.0)
    return (spike_clusters - speed_table).astype(jnp.float32)


def draw_kda_beta(key, part):
    key = jax.random.fold_in(key, 13)
    stochastic_seeds = jax.random.split(key, 4)
    patient_share = 0.5
    patient = jax.random.uniform(stochastic_seeds[0], (KDA_HEADS, 1), jnp.float32) < patient_share
    quick_base = jnp.exp(jax.random.uniform(stochastic_seeds[1], (KDA_HEADS, 1), jnp.float32, math.log(0.25), math.log(0.6)))
    patient_base = jnp.exp(jax.random.uniform(stochastic_seeds[2], (KDA_HEADS, 1), jnp.float32, math.log(0.3), math.log(0.6))) * HEAD_DIM / PROMPT_SPAN
    roughness = jnp.exp(jax.random.uniform(stochastic_seeds[3], (KDA_HEADS, PROMPT_SPAN), jnp.float32, math.log(0.5), math.log(1.5)))
    return (jnp.where(patient, patient_base, quick_base) * roughness).astype(jnp.float32)


def steps_of(key, shape, cuts, smallest, top_value):
    def one(position, blocks):
        draws = jax.random.uniform(jax.random.fold_in(jax.random.fold_in(key, 6), position), (blocks,), jnp.float32, smallest / len(cuts), top_value / len(cuts))
        return jnp.repeat(jnp.exp(draws), shape[position] // blocks).reshape((-1,) + (1,) * (len(shape) - position - 1))

    loudness = one(*cuts[0])
    for cut in cuts[1:]:
        loudness = loudness * one(*cut)
    return loudness


def gaussian(rng, dims, deviation, reach, pieces=(), kind=jnp.bfloat16):
    drawn = deviation * jax.random.normal(rng, dims, jnp.float32)
    if pieces:
        drawn = drawn * steps_of(rng, dims, pieces, -0.22, 0.18)
    return jnp.clip(drawn, -reach, reach).astype(kind)


def setup_inputs(seed: int = 0) -> dict:
    seeds = jax.random.split(jax.random.key(seed), 13)
    return {
        "mla_query": draw_mla_query(jax.random.fold_in(seeds[12], 71), 0),
        "mla_latent": draw_mla_latent(jax.random.fold_in(seeds[12], 71), 0),
        "kv_gain": jnp.clip(1.0 + 0.18 * jax.random.normal(seeds[2], (RANK,), jnp.float32), 0.1, 1.9),
        "w_key_up": gaussian(seeds[3], (RANK, MLA_HEADS * HEAD_DIM), RANK ** -0.5, 0.25, ((1, 4),)),
        "w_value_up": gaussian(seeds[4], (RANK, MLA_HEADS * HEAD_DIM), RANK ** -0.5, 0.25, ((1, 4),)),
        "w_mla_out": gaussian(seeds[5], (MLA_HEADS * HEAD_DIM, D), HEAD_DIM ** -0.5, 0.5, ((0, 4),)),
        "kda_query": gaussian(seeds[6], (PROMPT_SPAN, KDA_HEADS * HEAD_DIM), 1.0, 6.0, ((0, 64), (1, 4))),
        "kda_key": gaussian(seeds[7], (PROMPT_SPAN, KDA_HEADS * HEAD_DIM), 1.0, 6.0, ((0, 64), (1, 4))),
        "kda_value": gaussian(seeds[8], (PROMPT_SPAN, KDA_HEADS * HEAD_DIM), 1.0, 6.0, ((0, 64), (1, 4))),
        "kda_decay": draw_kda_decay(jax.random.fold_in(seeds[12], 71), 0),
        "kda_beta": draw_kda_beta(jax.random.fold_in(seeds[12], 71), 0),
        "w_kda_out": gaussian(seeds[11], (KDA_HEADS * HEAD_DIM, D), (KDA_HEADS * HEAD_DIM) ** -0.5, 0.125, ((0, 4),)),
    }


exact_mode = lax.Precision.HIGHEST

def held_bf16(values):
    return lax.optimization_barrier(values.astype(jnp.bfloat16)).astype(jnp.float32)

def unit_length(values):
    return values * lax.rsqrt(lax.optimization_barrier(jnp.sum(values * values, axis=-1, keepdims=True)) + 1e-06)

def latent_attention(mla_query, mla_latent, kv_gain, w_key_up, w_value_up, w_mla_out):
    row_width = HEAD_DIM + KEY_SHARED
    compressed = mla_latent[:, :RANK].astype(jnp.float32)
    normed = (compressed * lax.rsqrt(lax.optimization_barrier(jnp.mean(compressed * compressed, axis=1, keepdims=True)) + 1e-06) * kv_gain).astype(jnp.bfloat16)
    shared_key = mla_latent[:, RANK:].astype(jnp.float32)
    key_nope = held_bf16(jnp.dot(normed, w_key_up, preferred_element_type=jnp.float32)).reshape(PROMPT_SPAN, MLA_HEADS, HEAD_DIM)
    value_rows = held_bf16(jnp.dot(normed, w_value_up, preferred_element_type=jnp.float32)).reshape(PROMPT_SPAN, MLA_HEADS, HEAD_DIM)
    queries = mla_query.astype(jnp.float32).reshape(PROMPT_SPAN, MLA_HEADS, row_width)
    block_rows = math.gcd(PROMPT_SPAN, 256)
    key_position = jnp.arange(PROMPT_SPAN, dtype=jnp.int32)
    score_scale = 1.0 / math.sqrt(row_width)

    def query_block(block_index):
        picked = lax.dynamic_slice_in_dim(queries, block_index * block_rows, block_rows, 0)
        scores = jnp.einsum('qhd,khd->hqk', picked[:, :, :HEAD_DIM], key_nope, precision=exact_mode)
        scores = scores + jnp.einsum('qhd,kd->hqk', picked[:, :, HEAD_DIM:], shared_key, precision=exact_mode)
        scores = scores * score_scale
        query_position = block_index * block_rows + jnp.arange(block_rows, dtype=jnp.int32)
        visible = key_position[None, :] <= query_position[:, None]
        scores = jnp.where(visible[None], scores, -jnp.inf)
        row_peak = lax.optimization_barrier(jnp.max(scores, axis=2, keepdims=True))
        weights = jnp.exp(scores - row_peak)
        totals = lax.optimization_barrier(jnp.sum(weights, axis=2))
        blended = jnp.einsum('hqk,khd->qhd', held_bf16(weights), value_rows, precision=exact_mode)
        return blended / jnp.transpose(totals)[:, :, None]
    attended = lax.map(query_block, jnp.arange(PROMPT_SPAN // block_rows, dtype=jnp.int32))
    attended = attended.reshape(PROMPT_SPAN, MLA_HEADS * HEAD_DIM).astype(jnp.bfloat16)
    return jnp.dot(attended, w_mla_out, preferred_element_type=jnp.float32).astype(jnp.bfloat16)

def delta_layer(kda_query, kda_key, kda_value, kda_decay, kda_beta, w_kda_out):
    head_shape = (PROMPT_SPAN, KDA_HEADS, HEAD_DIM)
    unit_query = unit_length(kda_query.astype(jnp.float32).reshape(head_shape))
    unit_key = unit_length(kda_key.astype(jnp.float32).reshape(head_shape))
    value_heads = kda_value.astype(jnp.float32).reshape(head_shape)
    decay_heads = kda_decay.reshape(head_shape)
    strengths = jnp.transpose(kda_beta)

    def advance(carried, entries):
        query_row, key_row, value_row, decay_row, beta_row = entries
        decayed = jnp.exp(decay_row)[:, :, None] * carried
        recalled = jnp.einsum('hij,hi->hj', decayed, key_row, precision=exact_mode)
        mismatch = beta_row[:, None] * (value_row - recalled)
        carried = decayed + key_row[:, :, None] * mismatch[:, None, :]
        return (carried, jnp.einsum('hij,hi->hj', carried, query_row, precision=exact_mode))
    initial = jnp.zeros((KDA_HEADS, HEAD_DIM, HEAD_DIM), jnp.float32)
    _, produced = lax.scan(advance, initial, (unit_query, unit_key, value_heads, decay_heads, strengths))
    kda_heads = produced.reshape(PROMPT_SPAN, KDA_HEADS * HEAD_DIM).astype(jnp.bfloat16)
    return jnp.dot(kda_heads, w_kda_out, preferred_element_type=jnp.float32).astype(jnp.bfloat16)

def reference(mla_query, mla_latent, kv_gain, w_key_up, w_value_up, w_mla_out, kda_query, kda_key, kda_value, kda_decay, kda_beta, w_kda_out):
    mla_mixed = latent_attention(mla_query, mla_latent, kv_gain, w_key_up, w_value_up, w_mla_out)
    kda_mixed = delta_layer(kda_query, kda_key, kda_value, kda_decay, kda_beta, w_kda_out)
    return (mla_mixed, kda_mixed)
```

```python
import functools
import math

import jax
import jax.numpy as jnp
from jax import lax
from jax.experimental import pallas as pl
from jax.experimental.pallas import tpu as pltpu
from jax.sharding import PartitionSpec as P

HEAD_DIM = 128
KEY_SHARED = 64
SIDE = 4
HIDDEN_SCORE = -1e30
BF16 = jnp.bfloat16
F32 = jnp.float32
VMEM_LIMIT = 32 * 1024 * 1024


def call(kernel, out_shape, scratch=(), flops=0, num_in=0, scalars=0):
    single = isinstance(out_shape, jax.ShapeDtypeStruct)
    count = 1 if single else len(out_shape)
    specs = [pl.BlockSpec(memory_space=pltpu.SMEM)] * scalars
    specs += [pl.BlockSpec(memory_space=pltpu.VMEM)] * num_in
    out_specs = [pl.BlockSpec(memory_space=pltpu.VMEM)] * count
    return pl.pallas_call(
        kernel,
        out_shape=out_shape,
        in_specs=specs,
        out_specs=out_specs[0] if single else out_specs,
        scratch_shapes=list(scratch),
        compiler_params=pltpu.CompilerParams(vmem_limit_bytes=VMEM_LIMIT),
        cost_estimate=pl.CostEstimate(flops=flops, bytes_accessed=1 << 20, transcendentals=0),
    )


def struct(shape, dtype):
    return jax.ShapeDtypeStruct(shape, dtype)


def ctx_pairs(stride, by, wrap):
    pairs = []
    for index in range(SIDE**3):
        place = (index // stride) % SIDE
        target = place + by
        if wrap:
            target %= SIDE
        if 0 <= target < SIDE:
            pairs.append((index, index + (target - place) * stride))
    return pairs


def along(array, stride, by, wrap=True):
    return lax.ppermute(array, "ctx", ctx_pairs(stride, by, wrap))


def across_heads(array, flip):
    size = lax.axis_size("head")
    return lax.ppermute(array, "head", [(i, i ^ flip) for i in range(size)])


def dot(left, right):
    return jnp.dot(left, right, preferred_element_type=F32)


def dot_nt(left, right):
    return lax.dot_general(left, right, (((1,), (1,)), ((), ())), preferred_element_type=F32)


def split(values):
    high = values.astype(BF16)
    return high, (values - high.astype(F32)).astype(BF16)


def dot3(left, right, product=dot):
    left_high, left_low = split(left)
    right_high, right_low = split(right)
    return (
        product(left_high, right_high)
        + product(left_high, right_low)
        + product(left_low, right_high)
    )


def iota(shape, dim):
    return lax.broadcasted_iota(jnp.int32, shape, dim)


def unit_length(values):
    return values * lax.rsqrt(jnp.sum(values * values, axis=1, keepdims=True) + 1e-06)


def column_of(row):
    width = row.shape[1]
    square = jnp.where(
        iota((width, width), 0) == iota((width, width), 1), jnp.broadcast_to(row, (width, width)), 0.0
    )
    return jnp.sum(square, axis=1, keepdims=True)


def norm_kernel(latent_ref, gain_ref, out_ref):
    rank = gain_ref.shape[1]
    compressed = latent_ref[:, :rank].astype(F32)
    scale = lax.rsqrt(jnp.mean(compressed * compressed, axis=1, keepdims=True) + 1e-06)
    out_ref[:, :rank] = (compressed * scale * gain_ref[...]).astype(BF16)
    out_ref[:, rank:] = latent_ref[:, rank:]


def attend(carry_refs, place_ref, keys, slot_offset, q_refs, key_up_ref, value_up_ref):
    rank = key_up_ref.shape[0]
    head_count = key_up_ref.shape[1] // HEAD_DIM
    row_width = HEAD_DIM + KEY_SHARED
    key_count = keys[0].shape[0] * len(keys)
    query_count = q_refs[0].shape[0]
    exponent = math.log2(math.e) / math.sqrt(row_width)
    latent = jnp.concatenate([ref[...] for ref in keys], axis=0)
    nope = dot(latent[:, :rank], key_up_ref[...]).astype(BF16)
    value = dot(latent[:, :rank], value_up_ref[...]).astype(BF16)
    shared = latent[:, rank:]

    own_y, own_z, own_head = place_ref[1], place_ref[2], place_ref[3]
    rows = query_count // 4
    per_quarter = key_count // len(keys)
    index = iota((1, key_count), 1)
    quarter = own_head ^ (index // per_quarter + slot_offset)
    inside = index % per_quarter
    key_y = (own_y - inside // (rows * SIDE)) & (SIDE - 1)
    key_z = (own_z - (inside // rows) % SIDE) & (SIDE - 1)
    key_place = (key_y * SIDE + key_z) * query_count + quarter * rows + inside % rows
    query_place = (own_y * SIDE + own_z) * query_count + iota((query_count, 1), 0)
    visible = key_place <= query_place

    for head in range(head_count):
        lanes = slice(head * HEAD_DIM, (head + 1) * HEAD_DIM)
        head_keys = jnp.concatenate([nope[:, lanes], shared], axis=1)
        head_values = value[:, lanes]
        for chunk in range(SIDE):
            queries = q_refs[chunk][:, head * row_width : (head + 1) * row_width]
            scores = dot_nt(queries, head_keys)
            if chunk == 0:
                scores = jnp.where(visible, scores, HIDDEN_SCORE)
            top = jnp.max(scores, axis=1, keepdims=True)
            if carry_refs is not None:
                old_top = carry_refs[0][chunk, :, head : head + 1]
                top = jnp.maximum(top, old_top)
            weights = jnp.exp2((scores - top) * exponent)
            total = jnp.sum(weights, axis=1, keepdims=True)
            weighted = dot(weights.astype(BF16), head_values)
            if carry_refs is not None:
                keep = jnp.exp2((old_top - top) * exponent)
                total = total + keep * carry_refs[1][chunk, :, head : head + 1]
                weighted = weighted + keep * carry_refs[2][chunk, :, lanes]
            yield chunk, head, top, total, weighted


def attend_first_kernel(
    place_ref, own_ref, core_ref, q0, q1, q2, q3, key_up_ref, value_up_ref, top_ref, total_ref, sum_ref
):
    for chunk, head, top, total, weighted in attend(
        None, place_ref, (own_ref, core_ref), 0, (q0, q1, q2, q3), key_up_ref, value_up_ref
    ):
        top_ref[chunk, :, head : head + 1] = top
        total_ref[chunk, :, head : head + 1] = total
        sum_ref[chunk, :, head * HEAD_DIM : (head + 1) * HEAD_DIM] = weighted


def attend_last_kernel(
    place_ref, other_ref, cross_ref, q0, q1, q2, q3, key_up_ref, value_up_ref, top_ref, total_ref, sum_ref, out_ref
):
    width = sum_ref.shape[2]
    query_count = q0.shape[0]
    exponent = math.log2(math.e) / math.sqrt(HEAD_DIM + KEY_SHARED)
    lane = iota((query_count, HEAD_DIM), 1)
    packed = [jnp.zeros((query_count, HEAD_DIM), F32) for _ in range(SIDE)]
    for chunk, head, top, total, weighted in attend(
        (top_ref, total_ref, sum_ref),
        place_ref,
        (other_ref, cross_ref),
        2,
        (q0, q1, q2, q3),
        key_up_ref,
        value_up_ref,
    ):
        out_ref[chunk, :, head * HEAD_DIM : (head + 1) * HEAD_DIM] = (weighted / total).astype(BF16)
        level = top * exponent + jnp.log2(total)
        for part in range(3):
            piece = level.astype(BF16).astype(F32)
            level = level - piece
            packed[chunk] = jnp.where(lane == 3 * head + part, piece, packed[chunk])
    for chunk in range(SIDE):
        out_ref[chunk, :, width:] = packed[chunk].astype(BF16)


def merge_kernel(place_ref, own_ref, r1, r2, r3, w_ref, out_ref):
    own_x, own_head = place_ref[0], place_ref[3]
    width = w_ref.shape[0]
    parts = (own_ref[0], r1[...], r2[...], r3[...])
    levels = [part[:, width:].astype(F32) for part in parts]
    attended = []
    for head in range(width // HEAD_DIM):
        lanes = slice(head * HEAD_DIM, (head + 1) * HEAD_DIM)
        heights = []
        for behind in range(SIDE):
            height = (
                levels[behind][:, 3 * head : 3 * head + 1]
                + levels[behind][:, 3 * head + 1 : 3 * head + 2]
                + levels[behind][:, 3 * head + 2 : 3 * head + 3]
            )
            if behind:
                height = jnp.where(own_x >= behind, height, HIDDEN_SCORE)
            heights.append(height)
        top = functools.reduce(jnp.maximum, heights)
        shares = [jnp.exp2(height - top) for height in heights]
        total = sum(shares)
        blended = sum(
            share * part[:, lanes].astype(F32) for share, part in zip(shares, parts, strict=True)
        )
        attended.append((blended / total).astype(BF16))
    project(jnp.concatenate(attended, axis=1), w_ref, own_head, out_ref)


def project(rows, w_ref, own_head, out_ref):
    slots, _, columns = out_ref.shape
    projected = dot(rows, w_ref[...]).astype(BF16)
    for part in range(slots):
        out_ref[own_head ^ part] = projected[:, part * columns : (part + 1) * columns]


def sum_kernel(own_ref, r1, r2, r3, out_ref):
    out_ref[...] = (
        own_ref[0].astype(F32) + r1[...].astype(F32) + r2[...].astype(F32) + r3[...].astype(F32)
    ).astype(BF16)


def scattered_sum(pieces):
    received = [across_heads(pieces[flip], flip) for flip in range(1, 4)]
    return call(sum_kernel, struct(pieces.shape[1:], BF16), num_in=4)(pieces, *received)


def gather_latent(normed):
    rows = [normed] + [along(normed, 1, by) for by in range(1, SIDE)]
    rows = jnp.concatenate(rows, axis=0)
    rows = [rows] + [along(rows, SIDE, by) for by in range(1, SIDE)]
    return jnp.concatenate(rows, axis=0)


def delta_local_kernel(place_ref, key_ref, value_ref, decay_ref, beta_ref, go_ref, uw_ref, log_ref):
    own_z = place_ref[2]
    count, width = key_ref.shape
    head_count = width // HEAD_DIM
    row, col = iota((count, count), 0), iota((count, count), 1)
    ones = (col <= row).astype(BF16)
    decay = decay_ref[...]
    high = decay.astype(BF16)
    rest = decay - high.astype(F32)
    mid = rest.astype(BF16)
    low = (rest - mid.astype(F32)).astype(BF16)
    log_decay = dot(ones, high) + dot(ones, mid) + dot(ones, low)
    log_ref[...] = log_decay
    unit = (row == col).astype(F32)
    heads = range(head_count)
    negated, right_sides, ends, finals = [], [], [], []
    for head in heads:
        lanes = slice(head * HEAD_DIM, (head + 1) * HEAD_DIM)
        logs = log_decay[:, lanes]
        middle, last = logs[count // 2 - 1 : count // 2], logs[count - 1 :]
        keys = unit_length(key_ref[:, lanes].astype(F32))
        beta = column_of(beta_ref[head : head + 1, :])
        coupling = dot3(keys * jnp.exp(logs - middle), keys * jnp.exp(middle - logs), dot_nt)
        negated.append(jnp.where(col < row, coupling, 0.0) * beta)
        right_sides.append(
            jnp.concatenate(
                [beta * value_ref[:, lanes].astype(F32), beta * (keys * jnp.exp(logs))], axis=1
            )
        )
        ends.append(keys * jnp.exp(last - logs))
        finals.append(jnp.where(row == col, jnp.exp(last) - 1.0, 0.0))
    block = 1
    inverse = [None] * head_count
    while block < count:
        crossing = (row // (2 * block) == col // (2 * block)) & (row // block > col // block)
        below = [jnp.where(crossing, negated[head], 0.0) for head in heads]
        if block == 1:
            inverse = [unit - below[head] for head in heads]
        else:
            inner = [dot3(below[head], inverse[head]) for head in heads]
            inverse = [inverse[head] - dot3(inverse[head], inner[head]) for head in heads]
        block *= 2
    solved = [dot3(inverse[head], right_sides[head]) for head in heads]
    for head in heads:
        uw_ref[head] = solved[head]
        carried = dot3(jnp.transpose(ends[head]), solved[head])
        slot = (head - own_z) & (SIDE - 1)
        go_ref[slot, :HEAD_DIM, :] = (finals[head] - carried[:, HEAD_DIM:]).astype(BF16)
        go_ref[slot, HEAD_DIM:, :] = carried[:, :HEAD_DIM].astype(BF16)


def delta_reach_kernel(query_ref, key_ref, uw_ref, log_ref, gain_ref, offset_ref):
    count, width = key_ref.shape
    row, col = iota((count, count), 0), iota((count, count), 1)
    for head in range(width // HEAD_DIM):
        lanes = slice(head * HEAD_DIM, (head + 1) * HEAD_DIM)
        logs = log_ref[:, lanes]
        middle = logs[count // 2 - 1 : count // 2]
        keys = unit_length(key_ref[:, lanes].astype(F32))
        queries = unit_length(query_ref[:, lanes].astype(F32))
        reach = dot3(queries * jnp.exp(logs - middle), keys * jnp.exp(middle - logs), dot_nt)
        reach = jnp.where(col <= row, reach, 0.0)
        reached = dot3(reach, uw_ref[head])
        offset_ref[:, lanes] = reached[:, :HEAD_DIM]
        gain_ref[:, lanes] = queries * jnp.exp(logs) - reached[:, HEAD_DIM:]


def in_order(scratch, own_place, refs):
    for back, ref in enumerate(refs):
        scratch[(own_place - back) & (SIDE - 1)] = ref[...]


def carried_on(entry, state):
    high, low = split(state)
    step = entry[:HEAD_DIM]
    return state + entry[HEAD_DIM:].astype(F32) + (dot(step, high) + dot(step, low))


def compose(scratch):
    step = scratch[0, :HEAD_DIM, :].astype(F32)
    offset = scratch[0, HEAD_DIM:, :].astype(F32)
    for place in range(1, SIDE):
        entry = scratch[place]
        both = jnp.concatenate([step, offset], axis=1)
        high, low = split(both)
        moved = dot(entry[:HEAD_DIM], high) + dot(entry[:HEAD_DIM], low)
        step = step + entry[:HEAD_DIM].astype(F32) + moved[:, :HEAD_DIM]
        offset = offset + entry[HEAD_DIM:].astype(F32) + moved[:, HEAD_DIM:]
    return step, offset


def compose_first_kernel(place_ref, local_ref, r1, r2, r3, out_ref, scratch):
    in_order(scratch, place_ref[2], (local_ref.at[0], r1, r2, r3))
    step, offset = compose(scratch)
    out_ref[:HEAD_DIM, :] = step.astype(BF16)
    out_ref[HEAD_DIM:, :] = offset.astype(BF16)


def compose_second_kernel(place_ref, own_ref, r1, r2, r3, out_ref, scratch):
    in_order(scratch, place_ref[1], (own_ref, r1, r2, r3))
    step, offset = compose(scratch)
    out_ref[:HEAD_DIM, :] = step.astype(BF16)
    out_ref[HEAD_DIM:, :] = offset.astype(BF16)


def incoming_kernel(
    place_ref, local_ref, l1, l2, l3, own_ref, r1, r2, r3, x1, x2, x3, out_ref, by_z, by_y
):
    own_y, own_z = place_ref[1], place_ref[2]
    in_order(by_z, own_z, (local_ref.at[0], l1, l2, l3))
    in_order(by_y, own_y, (own_ref, r1, r2, r3))
    state = x3[HEAD_DIM:, :].astype(F32)
    for ref in (x2, x1):
        state = carried_on(ref[...], state)
    state = lax.fori_loop(0, own_y, lambda place, now: carried_on(by_y[place], now), state)
    for place in range(SIDE):
        out_ref[(place - own_z) & (SIDE - 1)] = state.astype(BF16)
        if place < SIDE - 1:
            state = carried_on(by_z[place], state)


def delta_out_kernel(place_ref, own_ref, r1, r2, r3, gain_ref, offset_ref, w_ref, out_ref, rows_ref):
    own_z, own_head = place_ref[2], place_ref[3]
    for back, ref in enumerate((own_ref.at[0], r1, r2, r3)):
        head = (own_z - back) & (SIDE - 1)
        lanes = pl.ds(pl.multiple_of(head * HEAD_DIM, HEAD_DIM), HEAD_DIM)
        high, low = split(gain_ref[:, lanes])
        state = ref[...]
        read = dot(high, state) + dot(low, state) + offset_ref[:, lanes]
        rows_ref[:, lanes] = read.astype(BF16)
    project(rows_ref[...], w_ref, own_head, out_ref)


def body(
    mla_query,
    mla_latent,
    kv_gain,
    w_key_up,
    w_value_up,
    w_mla_out,
    kda_query,
    kda_key,
    kda_value,
    kda_decay,
    kda_beta,
    w_kda_out,
):
    tokens, query_width = mla_query.shape
    width = w_key_up.shape[1]
    head_count = width // HEAD_DIM
    columns = w_mla_out.shape[1] // 4
    ctx = lax.axis_index("ctx")
    place = jnp.stack(
        [ctx // (SIDE * SIDE), (ctx // SIDE) % SIDE, ctx % SIDE, lax.axis_index("head")]
    ).astype(jnp.int32)
    square = (HEAD_DIM, HEAD_DIM)
    pair = (2 * HEAD_DIM, HEAD_DIM)

    with jax.named_scope("latent_gather"):
        normed = call(norm_kernel, struct(mla_latent.shape, BF16), num_in=2)(
            mla_latent, kv_gain[None, :]
        )
        quarter = gather_latent(normed)
        core_quarter = across_heads(quarter, 1)
        other_quarter = across_heads(quarter, 2)
        cross_quarter = across_heads(other_quarter, 1)
    with jax.named_scope("query_gather"):
        queries = [mla_query] + [
            along(mla_query, SIDE * SIDE, -by, wrap=False) for by in range(1, SIDE)
        ]

    with jax.named_scope("delta_local"):
        go, solved, logs = call(
            delta_local_kernel,
            (
                struct((SIDE,) + pair, BF16),
                struct((head_count, tokens, 2 * HEAD_DIM), F32),
                struct((tokens, width), F32),
            ),
            num_in=4,
            scalars=1,
            flops=10**9,
        )(place, kda_key, kda_value, kda_decay, kda_beta)
        local = [go] + [along(go[by], 1, by) for by in range(1, SIDE)]
        delta_gain, delta_offset = call(
            delta_reach_kernel,
            (struct((tokens, width), F32), struct((tokens, width), F32)),
            num_in=4,
            flops=10**9,
        )(kda_query, kda_key, solved, logs)
    with jax.named_scope("delta_scan"):
        chained = [pltpu.VMEM((SIDE,) + pair, BF16)]
        by_z = call(
            compose_first_kernel, struct(pair, BF16), chained, num_in=4, scalars=1, flops=10**8
        )(place, *local)
        by_z = [by_z] + [along(by_z, SIDE, by) for by in range(1, SIDE)]
        by_y = call(
            compose_second_kernel, struct(pair, BF16), chained, num_in=4, scalars=1, flops=10**8
        )(place, *by_z)
        by_x = [along(by_y, SIDE * SIDE, by, wrap=False) for by in range(1, SIDE)]
        states = call(
            incoming_kernel,
            struct((SIDE,) + square, BF16),
            chained * 2,
            num_in=11,
            scalars=1,
            flops=10**8,
        )(place, *local, *by_z, *by_x)
        states = [states] + [along(states[by], 1, by) for by in range(1, SIDE)]
    with jax.named_scope("delta_out"):
        delta_pieces = call(
            delta_out_kernel,
            struct((4, tokens, columns), BF16),
            [pltpu.VMEM((tokens, width), BF16)],
            num_in=7,
            scalars=1,
            flops=10**9,
        )(place, *states, delta_gain, delta_offset, w_kda_out)
        kda_mixed = scattered_sum(delta_pieces)

    with jax.named_scope("attend"):
        running = call(
            attend_first_kernel,
            (
                struct((SIDE, tokens, head_count), F32),
                struct((SIDE, tokens, head_count), F32),
                struct((SIDE, tokens, width), F32),
            ),
            num_in=8,
            scalars=1,
            flops=5 * 10**9,
        )(place, quarter, core_quarter, *queries, w_key_up, w_value_up)
        partial = call(
            attend_last_kernel,
            struct((SIDE, tokens, width + HEAD_DIM), BF16),
            num_in=11,
            scalars=1,
            flops=5 * 10**9,
        )(place, other_quarter, cross_quarter, *queries, w_key_up, w_value_up, *running)
        returned = [
            along(partial[by], SIDE * SIDE, by, wrap=False) for by in range(1, SIDE)
        ]
    with jax.named_scope("mla_out"):
        mla_pieces = call(
            merge_kernel, struct((4, tokens, columns), BF16), num_in=5, scalars=1, flops=10**9
        )(place, partial, *returned, w_mla_out)
        mla_mixed = scattered_sum(mla_pieces)
    return (mla_mixed, kda_mixed)


def solution(mesh):
    placed = (
        P("ctx", "head"),
        P(("ctx", "head"), None),
        P(),
        P(None, "head"),
        P(None, "head"),
        P("head", None),
        P("ctx", "head"),
        P("ctx", "head"),
        P("ctx", "head"),
        P("ctx", "head"),
        P("head", "ctx"),
        P("head", None),
    )
    return jax.shard_map(
        body,
        mesh=mesh,
        in_specs=placed,
        out_specs=(P("ctx", "head"), P("ctx", "head")),
        check_vma=False,
    )
```
